32 devices in a mesh: grp: 8 (over z, x), rep: 4 (over y, core).
Axes of the slice: x: 2, y: 2, z: 4, core: 2. Of those that a mesh axis runs over, the one named last changes fastest.
Arguments:
- activations: bfloat16 [32, 192, 6144], P(('grp', 'rep')), may hold values from -3 to 3
- cotangent: bfloat16 [32, 192, 6144], P(('grp', 'rep')), may hold values from -6 to 6
- documents: int32 [32, 192], P(('grp', 'rep')), may hold values from 0 to 3, never falling along the last dimension, each value on 1 to 96 neighbouring positions
- weight_copy: bfloat16 [6144, 256], P('grp'), may hold values from -0.078125 to 0.078125
- primary: float32 [6144, 256], P(('grp', 'rep')), may hold values from -0.0014648438 to 0.0014648438
- first_moment: float32 [6144, 256], P(('grp', 'rep')), may hold values from -1.5 to 1.5
- second_moment: float32 [6144, 256], P(('grp', 'rep')), may hold values from 0.001 to 0.1
Outputs:
- primary_new: float32 [6144, 256], P(('grp', 'rep'))
- first_new: float32 [6144, 256], P(('grp', 'rep'))
- second_new: float32 [6144, 256], P(('grp', 'rep'))
- copy_new: bfloat16 [6144, 256], P('grp')
The draws below stay inside these ranges and needn't reach their ends.
Inputs may be any that keep to these rules, and one draw needn't show every extreme that they name: Within each row of 192 tokens the document numbers never fall; each of the 4 documents has 1 to 96 tokens, and one has exactly 96.
All inputs are finite; a program needn't handle non-finite values.
Results may differ from the reference program's by a relative error of at most 0.015.
Values may be sent and summed in bfloat16 or wider, within the bound.
No kernel may reach another device: no remote copies, remote signals or barrier semaphores. Data moves between devices by JAX's collectives and lax.ppermute only.
A program may use at most 64 MiB of HBM per device.

```python
import math
import jax
import jax.numpy as jnp
import numpy as np
from jax import lax

D = 6144
TOK_DEV = 192
DOCS = 4
DOC_MOST = 96
ROWS = 32
TOKENS = 6144
COLS = 256


def strengthened(entries, stream_key, source, target, parts, factor):
    owner, partner = [(jnp.arange(entries.shape[dim]) // (entries.shape[dim] // parts)).reshape([-1 if axis == dim else 1 for axis in range(entries.ndim)]) for dim in (source, target)]
    chosen = jax.random.permutation(stream_key, parts)[partner]
    strong = (owner == chosen) | (owner == (partner + parts // 2) % parts)
    return jnp.where(strong, factor * entries, entries)


def level_of(key, extent, cuts, low, largest):
    gain, own = 1.0, jax.random.fold_in(key, 6)
    for axis_at, blocks in cuts:
        steps = jnp.exp(jax.random.uniform(jax.random.fold_in(own, axis_at), (blocks,), jnp.float32, low / len(cuts), largest / len(cuts)))
        gain = gain * jnp.repeat(steps, extent[axis_at] // blocks).reshape([-1 if axis == axis_at else 1 for axis in range(len(extent))])
    return gain


def profile(count, total, most, skew):
    weights = [(1 << 20) // math.isqrt(standing ** skew) + 1 for standing in range(2, count + 1)]
    spare, holding = total - most - (count - 1), [1] * (count - 1)
    while spare > 0:
        free = [i for i in range(count - 1) if holding[i] < most]
        mass, remaining = sum([weights[i] for i in free]), spare
        for i in free:
            extra = min(most - holding[i], max(1, remaining * weights[i] // mass), spare)
            holding[i] = holding[i] + extra
            spare = spare - extra
    return np.array([most] + holding)


def uneven_parts(key, count, total, bound, slope):
    if count == 2:
        one = jax.random.randint(key, (), max(1, total - bound), min(bound, total - 1) + 1)
        return jnp.stack([one, total - one])
    lengths = jnp.asarray(profile(count, total, bound, slope), jnp.int32)
    pairs = (count - 1) // 2
    source_of, receiver = lengths[1:1 + 2 * pairs:2], lengths[2:2 + 2 * pairs:2]
    margin = jnp.minimum(source_of - 1, bound - receiver)
    moved = jax.random.randint(jax.random.fold_in(key, 1), (pairs,), 0, 1 << 20) % (margin + 1)
    lengths = lengths.at[1:1 + 2 * pairs:2].set(source_of - moved).at[2:2 + 2 * pairs:2].set(receiver + moved)
    return lengths[jax.random.permutation(jax.random.fold_in(key, 2), count)]


def noise(own_key, dims, deviation, most, shards=(), held_as=jnp.bfloat16):
    array = deviation * jax.random.normal(own_key, dims, jnp.float32)
    if shards:
        array = array * level_of(own_key, dims, shards, -0.22, 0.18)
    return jnp.clip(array, -most, most).astype(held_as)


def gaussian_with(key, shape, width, bound, shards, heavy, held_as=jnp.bfloat16):
    drawn = width * jax.random.normal(key, shape, jnp.float32)
    if shards:
        drawn = drawn * level_of(key, shape, shards, -0.22, 0.18)
    return jnp.clip(strengthened(drawn, jax.random.fold_in(key, 3), *heavy), -bound, bound).astype(held_as)


def setup_inputs(seed: int = 0) -> dict:
    streams_of = jax.random.split(jax.random.key(seed), 8)
    activations = noise(streams_of[0], (ROWS, TOK_DEV, D), 1.0, 3.0, ((0, 32),))
    cotangent = gaussian_with(streams_of[1], (ROWS, TOK_DEV, D), 1.0, 6.0, ((0, 32),), (0, 2, 32, 2.75))
    documents = jax.vmap(lambda own: jnp.searchsorted(jnp.cumsum(uneven_parts(own, DOCS, TOK_DEV, DOC_MOST, 2)), jnp.arange(TOK_DEV), side="right"))(jax.random.split(streams_of[2], ROWS)).reshape((ROWS, TOK_DEV)).astype(jnp.int32)
    weight_copy = noise(streams_of[3], (D, COLS), D ** -0.5, 0.078125, ((0, 8),))
    primary = noise(streams_of[4], (D, COLS), 0.0001, 0.0014648438, ((0, 32),), jnp.float32)
    first_moment = noise(streams_of[5], (D, COLS), 0.1, 1.5, ((0, 32),), jnp.float32)
    second_moment = jnp.clip(jnp.exp(math.log(0.1) - 4.6051702 * jax.random.uniform(streams_of[6], (D, COLS), jnp.float32) ** level_of(streams_of[6], (D, COLS), ((0, 32),), -0.2, 0.2)), 0.001, 0.1)
    return dict(activations=activations, cotangent=cotangent, documents=documents, weight_copy=weight_copy, primary=primary, first_moment=first_moment, second_moment=second_moment)


BETA_FIRST = 0.9
BETA_SECOND = 0.95
LEARN_RATE = 6e-05
DECAY_RATE = 0.1
EPSILON = 1e-08
STEP_COUNT = 10.0

def row_gradient(features, cotan_row, doc_row, weight_copy, head_size):
    scale_value = 1.0 / math.sqrt(head_size)
    projected = jnp.dot(features, weight_copy[:, :3 * head_size], preferred_element_type=jnp.float32).astype(jnp.bfloat16)
    queries = projected[:, :head_size]
    key_rows = projected[:, head_size:2 * head_size]
    value_rows = projected[:, 2 * head_size:]
    scores = jnp.dot(queries, key_rows.T, preferred_element_type=jnp.float32) * scale_value
    token_count = features.shape[0]
    position = jnp.arange(token_count, dtype=jnp.int32)
    allowed = (position[None, :] <= position[:, None]) & (doc_row[None, :] == doc_row[:, None])
    exp_scores = jnp.where(allowed, jnp.exp(jnp.where(allowed, scores, 0.0)), 0.0)
    attention = exp_scores / lax.optimization_barrier(jnp.sum(exp_scores, axis=1, keepdims=True))
    attention_low = attention.astype(jnp.bfloat16)
    context = jnp.dot(attention_low, value_rows, preferred_element_type=jnp.float32).astype(jnp.bfloat16)
    back_context = jnp.dot(cotan_row, weight_copy[:, 3 * head_size:], preferred_element_type=jnp.float32).astype(jnp.bfloat16)
    back_attention = jnp.dot(back_context, value_rows.T, preferred_element_type=jnp.float32)
    back_values = jnp.dot(attention_low.T, back_context, preferred_element_type=jnp.float32).astype(jnp.bfloat16)
    inner_sum = lax.optimization_barrier(jnp.sum(attention * back_attention, axis=1, keepdims=True))
    back_scores = (attention * (back_attention - inner_sum) * scale_value).astype(jnp.bfloat16)
    back_queries = jnp.dot(back_scores, key_rows, preferred_element_type=jnp.float32).astype(jnp.bfloat16)
    back_keys = jnp.dot(back_scores.T, queries, preferred_element_type=jnp.float32).astype(jnp.bfloat16)
    back_projected = jnp.concatenate([back_queries, back_keys, back_values], axis=1)
    left_part = jnp.dot(features.T, back_projected, preferred_element_type=jnp.float32)
    right_part = jnp.dot(cotan_row.T, context, preferred_element_type=jnp.float32)
    return jnp.concatenate([left_part, right_part], axis=1)

def reference(activations, cotangent, documents, weight_copy, primary, first_moment, second_moment):
    head_size = weight_copy.shape[1] // 4
    grad_scale = 1.0 / math.sqrt(TOKENS)

    def accumulate(running_sum, row_items):
        features, cotan_row, doc_row = row_items
        row_term = row_gradient(features, cotan_row, doc_row, weight_copy, head_size) * grad_scale
        rounded = lax.optimization_barrier(row_term.astype(jnp.bfloat16)).astype(jnp.float32)
        return (running_sum + rounded, None)
    gradient, unused = lax.scan(accumulate, jnp.zeros(weight_copy.shape, jnp.float32), (activations, cotangent, documents))
    first_new = BETA_FIRST * first_moment + (1.0 - BETA_FIRST) * gradient
    second_new = BETA_SECOND * second_moment + (1.0 - BETA_SECOND) * gradient * gradient
    correct_first = 1.0 - BETA_FIRST ** STEP_COUNT
    correct_second = 1.0 - BETA_SECOND ** STEP_COUNT
    update = first_new / correct_first / (jnp.sqrt(second_new / correct_second) + EPSILON)
    primary_new = primary - LEARN_RATE * (update + DECAY_RATE * primary)
    copy_new = primary_new.astype(jnp.bfloat16)
    return (primary_new, first_new, second_new, copy_new)
```

```python
import functools
import math

import jax
import jax.numpy as jnp
from jax import lax
from jax.experimental import pallas as pl
from jax.experimental.pallas import tpu as pltpu
from jax.sharding import PartitionSpec as P

BETA_FIRST = 0.9
BETA_SECOND = 0.95
LEARN_RATE = 6e-05
DECAY_RATE = 0.1
EPSILON = 1e-08
STEP_COUNT = 10.0

AXES = ("grp", "rep")
MIB = 1024 * 1024


def adam(gradient, primary, first_moment, second_moment):
    first_new = BETA_FIRST * first_moment + (1.0 - BETA_FIRST) * gradient
    second_new = BETA_SECOND * second_moment + (1.0 - BETA_SECOND) * gradient * gradient
    correct_first = 1.0 - BETA_FIRST**STEP_COUNT
    correct_second = 1.0 - BETA_SECOND**STEP_COUNT
    update = first_new / correct_first / (jnp.sqrt(second_new / correct_second) + EPSILON)
    primary_new = primary - LEARN_RATE * (update + DECAY_RATE * primary)
    return primary_new, first_new, second_new


def plain_body(activations, cotangent, documents, weight_copy, primary, first_moment, second_moment):
    features = activations[0]
    cotan_rows = cotangent[0]
    doc_row = documents[0]
    head = weight_copy.shape[1] // 4
    token_count = features.shape[0]
    grad_scale = 1.0 / math.sqrt(lax.axis_size("grp") * lax.axis_size("rep") * token_count)
    scale_value = 1.0 / math.sqrt(head)
    dot = functools.partial(jnp.dot, preferred_element_type=jnp.float32)
    weights = lax.all_gather(weight_copy, "grp", axis=0, tiled=True)
    projected = dot(features, weights[:, : 3 * head]).astype(jnp.bfloat16)
    back_context = dot(cotan_rows, weights[:, 3 * head :]).astype(jnp.bfloat16)
    queries, key_rows, value_rows = jnp.split(projected, 3, axis=1)
    scores = dot(queries, key_rows.T) * scale_value
    position = jnp.arange(token_count, dtype=jnp.int32)
    allowed = (position[None, :] <= position[:, None]) & (doc_row[None, :] == doc_row[:, None])
    exp_scores = jnp.where(allowed, jnp.exp(jnp.where(allowed, scores, 0.0)), 0.0)
    attention = exp_scores / jnp.sum(exp_scores, axis=1, keepdims=True)
    attention_low = attention.astype(jnp.bfloat16)
    context = dot(attention_low, value_rows).astype(jnp.bfloat16)
    back_attention = dot(back_context, value_rows.T)
    back_values = dot(attention_low.T, back_context).astype(jnp.bfloat16)
    inner_sum = jnp.sum(attention * back_attention, axis=1, keepdims=True)
    back_scores = (attention * (back_attention - inner_sum) * scale_value).astype(jnp.bfloat16)
    back_queries = dot(back_scores, key_rows).astype(jnp.bfloat16)
    back_keys = dot(back_scores.T, queries).astype(jnp.bfloat16)
    back_projected = jnp.concatenate([back_queries, back_keys, back_values], axis=1)
    term = jnp.concatenate([dot(features.T, back_projected), dot(cotan_rows.T, context)], axis=1)
    term = (term * grad_scale).astype(jnp.bfloat16)
    partial_sum = lax.psum_scatter(term, "grp", scatter_dimension=0, tiled=True)
    gradient = lax.psum_scatter(partial_sum, "rep", scatter_dimension=0, tiled=True)
    primary_new, first_new, second_new = adam(
        gradient.astype(jnp.float32), primary, first_moment, second_moment
    )
    copy_new = lax.all_gather(primary_new.astype(jnp.bfloat16), "rep", axis=0, tiled=True)
    return primary_new, first_new, second_new, copy_new


def hop(value, kz, kx, ky, kc):
    offset = (kz * 2 + kx) * 4 + ky * 2 + kc
    return lax.ppermute(value, AXES, [(i, i ^ offset) for i in range(32)])


def join(*parts):
    return jnp.concatenate(parts, axis=0)


def block_start(kz, kx, ky, kc, rows):
    me = lax.axis_index("grp") * 4 + lax.axis_index("rep")
    offset = (kz * 2 + kx) * 4 + ky * 2 + kc
    return pl.multiple_of(lax.bitwise_xor(me, jnp.int32(offset)) * rows, rows)


def turn_kernel(a_ref, b_ref, at_ref, bt_ref, *, step):
    for source, target in ((a_ref, at_ref), (b_ref, bt_ref)):
        for start in range(0, source.shape[1], step):
            target[start : start + step, :] = source[:, start : start + step].T


def fdot(a, b, dims):
    return lax.dot_general(a, b, (dims, ((), ())), preferred_element_type=jnp.float32)


MM = ((1,), (0,))
MT = ((1,), (1,))
TM = ((0,), (0,))


def attend_kernel(places, rows, head, grad_scale, *refs):
    count = len(places)
    pieces = refs[:count]
    acts, cots, doc_row, doc_col, acts_t, cots_t = refs[count : count + 6]
    other_ref, left_ref, right_ref = refs[count + 6 : count + 9]
    weights = refs[count + 9]
    for piece, place in zip(pieces, places):
        for index, where in enumerate(place):
            if where is None:
                size = piece.shape[0]
                start = pl.multiple_of(lax.axis_index("grp") * size, size)
                weights[pl.ds(start, size), :] = piece[...]
            else:
                weights[pl.ds(block_start(*where, rows), rows), :] = piece[
                    index * rows : (index + 1) * rows, :
                ]
    projected = fdot(acts[...], weights[:, : 3 * head], MM).astype(jnp.bfloat16)
    back_context = fdot(cots[...], weights[:, 3 * head :], MM).astype(jnp.bfloat16)
    queries = projected[:, :head]
    key_rows = projected[:, head : 2 * head]
    value_rows = projected[:, 2 * head :]
    scale_value = 1.0 / math.sqrt(head)
    scores = fdot(queries, key_rows, MT) * scale_value
    tokens = scores.shape[0]
    here = lax.broadcasted_iota(jnp.int32, (tokens, tokens), 0)
    there = lax.broadcasted_iota(jnp.int32, (tokens, tokens), 1)
    allowed = (there <= here) & (doc_row[...] == doc_col[...])
    exp_scores = jnp.where(allowed, jnp.exp(jnp.where(allowed, scores, 0.0)), 0.0)
    attention = exp_scores / jnp.sum(exp_scores, axis=1, keepdims=True)
    attention_low = attention.astype(jnp.bfloat16)
    context = fdot(attention_low, value_rows, MM).astype(jnp.bfloat16)
    back_attention = fdot(back_context, value_rows, MT)
    back_values = fdot(attention_low, back_context, TM).astype(jnp.bfloat16)
    inner_sum = jnp.sum(attention * back_attention, axis=1, keepdims=True)
    back_scores = (attention * (back_attention - inner_sum) * scale_value).astype(jnp.bfloat16)
    back_queries = fdot(back_scores, key_rows, MM).astype(jnp.bfloat16)
    back_keys = fdot(back_scores, queries, TM).astype(jnp.bfloat16)
    none = jnp.zeros((tokens, head), jnp.bfloat16)
    left = jnp.concatenate([back_queries, back_keys, back_values, none], axis=1)
    right = jnp.concatenate([none, none, none, context], axis=1)
    left_ref[...] = left
    right_ref[...] = right
    write_terms(acts_t, cots_t, left, right, other_ref, 1, rows, grad_scale)


def write_terms(acts_t, cots_t, left, right, out_ref, kc, rows, grad_scale):
    for index in range(16):
        start = block_start(index // 4, index // 2 % 2, index % 2, kc, rows)
        term = fdot(acts_t[pl.ds(start, rows), :], left, MM)
        term += fdot(cots_t[pl.ds(start, rows), :], right, MM)
        out_ref[index * rows : (index + 1) * rows, :] = (term * grad_scale).astype(out_ref.dtype)


def mine_kernel(rows, grad_scale, acts_t, cots_t, left_ref, right_ref, out_ref):
    write_terms(acts_t, cots_t, left_ref[...], right_ref[...], out_ref, 0, rows, grad_scale)


def vmem(count):
    return [pl.BlockSpec(memory_space=pltpu.VMEM)] * count


def kernel_call(body, outs, name, args, scratch=(), flops=0, limit=24):
    return pl.pallas_call(
        body,
        out_shape=outs,
        in_specs=vmem(len(args)),
        out_specs=vmem(len(outs)),
        scratch_shapes=scratch,
        name=name,
        compiler_params=pltpu.CompilerParams(vmem_limit_bytes=limit * MIB),
        cost_estimate=pl.CostEstimate(flops=flops, bytes_accessed=4 * MIB, transcendentals=0),
    )(*args)


def gather(weight_copy, rows):
    rep = lax.axis_index("rep")
    own = lax.dynamic_slice_in_dim(weight_copy, rep * rows, rows, 0)
    half = lax.dynamic_slice_in_dim(weight_copy, jnp.bitwise_xor(rep, 2) * rows, rows, 0)
    z2 = hop(own, 2, 0, 0, 0)
    z1 = hop(own, 1, 0, 0, 0)
    x0 = hop(join(own, half), 0, 1, 0, 0)
    z12 = join(z1, z2)
    z3 = hop(z2, 1, 0, 0, 0)
    x12 = hop(z12, 0, 1, 0, 0)
    y12 = hop(z12, 0, 0, 1, 0)
    c0 = hop(join(z12, x0), 0, 0, 0, 1)
    x3 = hop(z3, 0, 1, 0, 0)
    ya = hop(join(z3, x12), 0, 0, 1, 0)
    c1 = hop(join(z3, x12, y12), 0, 0, 0, 1)
    yb = hop(x3, 0, 0, 1, 0)
    c2 = hop(join(x3, ya, yb), 0, 0, 0, 1)
    z12_at = [(1, 0, 0), (2, 0, 0)]
    x0_at = [(0, 1, 0), (0, 1, 1)]
    x12_at = [(1, 1, 0), (2, 1, 0)]
    y12_at = [(1, 0, 1), (2, 0, 1)]
    z3_at, x3_at, yb_at = [(3, 0, 0)], [(3, 1, 0)], [(3, 1, 1)]
    ya_at = [(3, 0, 1), (1, 1, 1), (2, 1, 1)]

    def core(kc, *lists):
        return [(*at, kc) for one in lists for at in one]

    return [
        (weight_copy, [None]),
        (z12, core(0, z12_at)),
        (x0, core(0, x0_at)),
        (z3, core(0, z3_at)),
        (x12, core(0, x12_at)),
        (y12, core(0, y12_at)),
        (x3, core(0, x3_at)),
        (ya, core(0, ya_at)),
        (yb, core(0, yb_at)),
        (c0, core(1, z12_at, x0_at)),
        (c1, core(1, z3_at, x12_at, y12_at)),
        (c2, core(1, x3_at, ya_at, yb_at)),
    ]


def scatter(mine, other, rows):
    received = hop(other, 0, 0, 0, 1)

    def block(kz, kx, ky):
        start = ((kz * 2 + kx) * 2 + ky) * rows
        both = mine[start : start + rows] + received[start : start + rows].astype(jnp.float32)
        return both

    def send(at, kz, kx, ky):
        return hop(join(*[block(*one).astype(jnp.bfloat16) for one in at]), kz, kx, ky, 0)

    got = {}
    for pair in ((3, 2), (1, 0)):
        for kx, ky in ((1, 1), (1, 0), (0, 1)):
            came = send([(kz, kx, ky) for kz in pair], 0, kx, ky)
            for index, kz in enumerate(pair):
                got.setdefault(kz, []).append(came[index * rows : (index + 1) * rows])
    totals = {kz: block(kz, 0, 0) + sum(one.astype(jnp.float32) for one in got[kz]) for kz in got}
    gradient = totals[0]
    for kz in (3, 2, 1):
        gradient += hop(totals[kz].astype(jnp.bfloat16), kz, 0, 0, 0).astype(jnp.float32)
    return gradient


def block_body(activations, cotangent, documents, weight_copy, primary, first_moment, second_moment):
    acts, cots = activations[0], cotangent[0]
    tokens, depth = acts.shape
    columns = weight_copy.shape[1]
    rows = primary.shape[0]
    head = columns // 4
    grad_scale = 1.0 / math.sqrt(32 * tokens)
    turned = jax.ShapeDtypeStruct((depth, tokens), jnp.bfloat16)
    acts_t, cots_t = kernel_call(
        functools.partial(turn_kernel, step=512), [turned, turned], "turn", (acts, cots)
    )
    pieces = gather(weight_copy, rows)
    places = [place for _, place in pieces]
    side = jax.ShapeDtypeStruct((tokens, columns), jnp.bfloat16)
    other, left, right = kernel_call(
        functools.partial(attend_kernel, places, rows, head, grad_scale),
        [jax.ShapeDtypeStruct((16 * rows, columns), jnp.bfloat16), side, side],
        "attend",
        (
            *[piece for piece, _ in pieces],
            acts,
            cots,
            documents,
            documents.reshape(tokens, 1),
            acts_t,
            cots_t,
        ),
        scratch=[pltpu.VMEM((depth, columns), jnp.bfloat16)],
        flops=4 * tokens * depth * columns,
        limit=32,
    )
    (mine,) = kernel_call(
        functools.partial(mine_kernel, rows, grad_scale),
        [jax.ShapeDtypeStruct((16 * rows, columns), jnp.float32)],
        "mine",
        (acts_t, cots_t, left, right),
        flops=2 * tokens * depth * columns,
    )
    gradient = scatter(mine, other, rows)
    primary_new, first_new, second_new = adam(gradient, primary, first_moment, second_moment)
    copy_new = lax.all_gather(primary_new.astype(jnp.bfloat16), "rep", axis=0, tiled=True)
    return primary_new, first_new, second_new, copy_new


def chosen_body(activations, cotangent, documents, weight_copy, primary, first_moment, second_moment):
    blocks = lax.axis_size("grp") == 8 and lax.axis_size("rep") == 4
    tiled = primary.shape[0] % 16 == 0 and activations.shape[1] % 16 == 0
    args = (activations, cotangent, documents, weight_copy, primary, first_moment, second_moment)
    return block_body(*args) if blocks and tiled else plain_body(*args)


def solution(mesh):
    in_specs = (
        P(("grp", "rep"), None, None),
        P(("grp", "rep"), None, None),
        P(("grp", "rep"), None),
        P("grp", None),
        P(("grp", "rep"), None),
        P(("grp", "rep"), None),
        P(("grp", "rep"), None),
    )
    out_specs = (
        P(("grp", "rep"), None),
        P(("grp", "rep"), None),
        P(("grp", "rep"), None),
        P("grp", None),
    )
    return jax.shard_map(chosen_body, mesh=mesh, in_specs=in_specs, out_specs=out_specs, check_vma=False)
```

```python
import functools
import math

import jax
import jax.numpy as jnp
from jax import lax
from jax.experimental import pallas as pl
from jax.experimental.pallas import tpu as pltpu
from jax.sharding import PartitionSpec as P

BETA_FIRST = 0.9
BETA_SECOND = 0.95
LEARN_RATE = 6e-05
DECAY_RATE = 0.1
EPSILON = 1e-08
STEP_COUNT = 10.0

AXES = ("grp", "rep")
MIB = 1024 * 1024
FAR = (2, 3)
NEAR = (1, 0)


def adam(gradient, primary, first_moment, second_moment):
    first_new = BETA_FIRST * first_moment + (1.0 - BETA_FIRST) * gradient
    second_new = BETA_SECOND * second_moment + (1.0 - BETA_SECOND) * gradient * gradient
    correct_first = 1.0 - BETA_FIRST**STEP_COUNT
    correct_second = 1.0 - BETA_SECOND**STEP_COUNT
    update = first_new / correct_first / (jnp.sqrt(second_new / correct_second) + EPSILON)
    primary_new = primary - LEARN_RATE * (update + DECAY_RATE * primary)
    return primary_new, first_new, second_new


def plain_body(activations, cotangent, documents, weight_copy, primary, first_moment, second_moment):
    features = activations[0]
    cotan_rows = cotangent[0]
    doc_row = documents[0]
    head = weight_copy.shape[1] // 4
    token_count = features.shape[0]
    grad_scale = 1.0 / math.sqrt(lax.axis_size("grp") * lax.axis_size("rep") * token_count)
    scale_value = 1.0 / math.sqrt(head)
    dot = functools.partial(jnp.dot, preferred_element_type=jnp.float32)
    weights = lax.all_gather(weight_copy, "grp", axis=0, tiled=True)
    projected = dot(features, weights[:, : 3 * head]).astype(jnp.bfloat16)
    back_context = dot(cotan_rows, weights[:, 3 * head :]).astype(jnp.bfloat16)
    queries, key_rows, value_rows = jnp.split(projected, 3, axis=1)
    scores = dot(queries, key_rows.T) * scale_value
    position = jnp.arange(token_count, dtype=jnp.int32)
    allowed = (position[None, :] <= position[:, None]) & (doc_row[None, :] == doc_row[:, None])
    exp_scores = jnp.where(allowed, jnp.exp(jnp.where(allowed, scores, 0.0)), 0.0)
    attention = exp_scores / jnp.sum(exp_scores, axis=1, keepdims=True)
    attention_low = attention.astype(jnp.bfloat16)
    context = dot(attention_low, value_rows).astype(jnp.bfloat16)
    back_attention = dot(back_context, value_rows.T)
    back_values = dot(attention_low.T, back_context).astype(jnp.bfloat16)
    inner_sum = jnp.sum(attention * back_attention, axis=1, keepdims=True)
    back_scores = (attention * (back_attention - inner_sum) * scale_value).astype(jnp.bfloat16)
    back_queries = dot(back_scores, key_rows).astype(jnp.bfloat16)
    back_keys = dot(back_scores.T, queries).astype(jnp.bfloat16)
    back_projected = jnp.concatenate([back_queries, back_keys, back_values], axis=1)
    term = jnp.concatenate([dot(features.T, back_projected), dot(cotan_rows.T, context)], axis=1)
    term = (term * grad_scale).astype(jnp.bfloat16)
    partial_sum = lax.psum_scatter(term, "grp", scatter_dimension=0, tiled=True)
    gradient = lax.psum_scatter(partial_sum, "rep", scatter_dimension=0, tiled=True)
    primary_new, first_new, second_new = adam(
        gradient.astype(jnp.float32), primary, first_moment, second_moment
    )
    copy_new = lax.all_gather(primary_new.astype(jnp.bfloat16), "rep", axis=0, tiled=True)
    return primary_new, first_new, second_new, copy_new


def hop(value, kz, kx, ky, kc):
    offset = (kz * 2 + kx) * 4 + ky * 2 + kc
    return lax.ppermute(value, AXES, [(i, i ^ offset) for i in range(32)])


def join(*parts):
    return jnp.concatenate(parts, axis=0)


def block_start(kz, kx, ky, kc, rows):
    me = lax.axis_index("grp") * 4 + lax.axis_index("rep")
    offset = (kz * 2 + kx) * 4 + ky * 2 + kc
    return pl.multiple_of(lax.bitwise_xor(me, jnp.int32(offset)) * rows, rows)


def turn_kernel(a_ref, b_ref, at_ref, bt_ref, *, step):
    for source, target in ((a_ref, at_ref), (b_ref, bt_ref)):
        for start in range(0, source.shape[1], step):
            target[start : start + step, :] = source[:, start : start + step].T


def fdot(a, b, dims):
    return lax.dot_general(a, b, (dims, ((), ())), preferred_element_type=jnp.float32)


MM = ((1,), (0,))
MT = ((1,), (1,))
TM = ((0,), (0,))


def attend_kernel(places, rows, head, grad_scale, *refs):
    count = len(places)
    pieces = refs[:count]
    acts, cots, docs, acts_t, cots_t = refs[count : count + 5]
    far_ref, near_ref, left_ref, right_ref, weights = refs[count + 5 :]
    for piece, place in zip(pieces, places):
        for index, where in enumerate(place):
            if where is None:
                size = piece.shape[0]
                start = pl.multiple_of(lax.axis_index("grp") * size, size)
                weights[pl.ds(start, size), :] = piece[...]
            else:
                weights[pl.ds(block_start(*where, rows), rows), :] = piece[
                    index * rows : (index + 1) * rows, :
                ]
    projected = fdot(acts[...], weights[:, : 3 * head], MM).astype(jnp.bfloat16)
    back_context = fdot(cots[...], weights[:, 3 * head :], MM).astype(jnp.bfloat16)
    queries = projected[:, :head]
    key_rows = projected[:, head : 2 * head]
    value_rows = projected[:, 2 * head :]
    scale_value = 1.0 / math.sqrt(head)
    scores = fdot(queries, key_rows, MT) * scale_value
    tokens = scores.shape[0]
    here = lax.broadcasted_iota(jnp.int32, (tokens, tokens), 0)
    there = lax.broadcasted_iota(jnp.int32, (tokens, tokens), 1)
    document = jnp.broadcast_to(docs[...], (tokens, tokens))
    allowed = (there <= here) & (document == document.T)
    exp_scores = jnp.where(allowed, jnp.exp(jnp.where(allowed, scores, 0.0)), 0.0)
    attention = exp_scores / jnp.sum(exp_scores, axis=1, keepdims=True)
    attention_low = attention.astype(jnp.bfloat16)
    context = fdot(attention_low, value_rows, MM).astype(jnp.bfloat16)
    back_attention = fdot(back_context, value_rows, MT)
    back_values = fdot(attention_low, back_context, TM).astype(jnp.bfloat16)
    inner_sum = jnp.sum(attention * back_attention, axis=1, keepdims=True)
    back_scores = (attention * (back_attention - inner_sum) * scale_value).astype(jnp.bfloat16)
    back_queries = fdot(back_scores, key_rows, MM).astype(jnp.bfloat16)
    back_keys = fdot(back_scores, queries, TM).astype(jnp.bfloat16)
    none = jnp.zeros((tokens, head), jnp.bfloat16)
    left = jnp.concatenate([back_queries, back_keys, back_values, none], axis=1)
    right = jnp.concatenate([none, none, none, context], axis=1)
    left_ref[...] = left
    right_ref[...] = right
    write_terms(acts_t, cots_t, left, right, far_ref, FAR, 1, rows, grad_scale)
    write_terms(acts_t, cots_t, left, right, near_ref, NEAR, 1, rows, grad_scale)


def write_terms(acts_t, cots_t, left, right, out_ref, kzs, kc, rows, grad_scale):
    for index, (kz, kx, ky) in enumerate((kz, kx, ky) for kz in kzs for kx in (0, 1) for ky in (0, 1)):
        start = block_start(kz, kx, ky, kc, rows)
        term = fdot(acts_t[pl.ds(start, rows), :], left, MM)
        term += fdot(cots_t[pl.ds(start, rows), :], right, MM)
        out_ref[index * rows : (index + 1) * rows, :] = (term * grad_scale).astype(out_ref.dtype)


def mine_kernel(kzs, rows, grad_scale, acts_t, cots_t, left_ref, right_ref, out_ref):
    write_terms(acts_t, cots_t, left_ref[...], right_ref[...], out_ref, kzs, 0, rows, grad_scale)


def vmem(count):
    return [pl.BlockSpec(memory_space=pltpu.VMEM)] * count


def kernel_call(body, outs, name, args, scratch=(), flops=0, limit=16):
    return pl.pallas_call(
        body,
        out_shape=outs,
        in_specs=vmem(len(args)),
        out_specs=vmem(len(outs)),
        scratch_shapes=scratch,
        name=name,
        compiler_params=pltpu.CompilerParams(vmem_limit_bytes=limit * MIB),
        cost_estimate=pl.CostEstimate(flops=flops, bytes_accessed=4 * MIB, transcendentals=0),
    )(*args)


def gather(weight_copy, rows, beside):
    rep = lax.axis_index("rep")
    own = lax.dynamic_slice_in_dim(weight_copy, rep * rows, rows, 0)
    half = lax.dynamic_slice_in_dim(weight_copy, jnp.bitwise_xor(rep, 2) * rows, rows, 0)
    both = join(own, half)
    z2 = hop(own, 2, 0, 0, 0)
    z1 = hop(both, 1, 0, 0, 0)
    x0 = hop(both, 0, 1, 0, 0)
    zx = hop(both, 1, 1, 0, 0)
    z2, *beside = lax.optimization_barrier((z2, *beside))
    z3 = hop(z2, 1, 0, 0, 0)
    x2 = hop(z2, 0, 1, 0, 0)
    y2 = hop(z2, 0, 0, 1, 0)
    x3 = hop(z3, 0, 1, 0, 0)
    ya = hop(join(z3, x2), 0, 0, 1, 0)
    yb = hop(x3, 0, 0, 1, 0)
    c0 = hop(join(z1, x0, zx), 0, 0, 0, 1)
    c1 = hop(join(z2, z3, x2, y2), 0, 0, 0, 1)
    c2 = hop(join(x3, ya, yb), 0, 0, 0, 1)
    z1_at = [(1, 0, 0), (1, 0, 1)]
    x0_at = [(0, 1, 0), (0, 1, 1)]
    zx_at = [(1, 1, 0), (1, 1, 1)]
    z2_at, z3_at, x2_at, y2_at = [(2, 0, 0)], [(3, 0, 0)], [(2, 1, 0)], [(2, 0, 1)]
    x3_at, yb_at = [(3, 1, 0)], [(3, 1, 1)]
    ya_at = [(3, 0, 1), (2, 1, 1)]

    def core(kc, *lists):
        return [(*at, kc) for one in lists for at in one]

    pieces = [
        (weight_copy, [None]),
        (z1, core(0, z1_at)),
        (x0, core(0, x0_at)),
        (zx, core(0, zx_at)),
        (z2, core(0, z2_at)),
        (z3, core(0, z3_at)),
        (x2, core(0, x2_at)),
        (y2, core(0, y2_at)),
        (x3, core(0, x3_at)),
        (ya, core(0, ya_at)),
        (yb, core(0, yb_at)),
        (c0, core(1, z1_at, x0_at, zx_at)),
        (c1, core(1, z2_at, z3_at, x2_at, y2_at)),
        (c2, core(1, x3_at, ya_at, yb_at)),
    ]
    return pieces, beside


def plane_sum(mine, received, kzs, rows):
    def block(kz, kx, ky):
        start = ((kzs.index(kz) * 2 + kx) * 2 + ky) * rows
        return mine[start : start + rows] + received[start : start + rows].astype(jnp.float32)

    totals = [block(kz, 0, 0) for kz in kzs]
    for kx, ky in ((1, 1), (1, 0), (0, 1)):
        came = hop(join(*[block(kz, kx, ky).astype(jnp.bfloat16) for kz in kzs]), 0, kx, ky, 0)
        for index in range(len(kzs)):
            totals[index] += came[index * rows : (index + 1) * rows].astype(jnp.float32)
    return totals


def block_body(activations, cotangent, documents, weight_copy, primary, first_moment, second_moment):
    acts, cots = activations[0], cotangent[0]
    tokens, depth = acts.shape
    columns = weight_copy.shape[1]
    rows = primary.shape[0]
    head = columns // 4
    grad_scale = 1.0 / math.sqrt(32 * tokens)
    turned = jax.ShapeDtypeStruct((depth, tokens), jnp.bfloat16)
    acts_t, cots_t = kernel_call(
        functools.partial(turn_kernel, step=512), [turned, turned], "turn", (acts, cots)
    )
    pieces, (acts_t, cots_t) = gather(weight_copy, rows, (acts_t, cots_t))
    places = [place for _, place in pieces]
    side = jax.ShapeDtypeStruct((tokens, columns), jnp.bfloat16)
    other = jax.ShapeDtypeStruct((8 * rows, columns), jnp.bfloat16)
    far, near, left, right = kernel_call(
        functools.partial(attend_kernel, places, rows, head, grad_scale),
        [other, other, side, side],
        "attend",
        (*[piece for piece, _ in pieces], acts, cots, documents, acts_t, cots_t),
        scratch=[pltpu.VMEM((depth, columns), jnp.bfloat16)],
        flops=4 * tokens * depth * columns,
    )
    totals = {}
    for kzs, sent in ((FAR, far), (NEAR, near)):
        received = hop(sent, 0, 0, 0, 1)
        (mine,) = kernel_call(
            functools.partial(mine_kernel, kzs, rows, grad_scale),
            [jax.ShapeDtypeStruct((8 * rows, columns), jnp.float32)],
            "mine",
            (acts_t, cots_t, left, right),
            flops=tokens * depth * columns,
        )
        totals.update(zip(kzs, plane_sum(mine, received, kzs, rows)))
    gradient = totals[0]
    for kz in (2, 3, 1):
        gradient += hop(totals[kz].astype(jnp.bfloat16), kz, 0, 0, 0).astype(jnp.float32)
    primary_new, first_new, second_new = adam(gradient, primary, first_moment, second_moment)
    copy_new = lax.all_gather(primary_new.astype(jnp.bfloat16), "rep", axis=0, tiled=True)
    return primary_new, first_new, second_new, copy_new


def chosen_body(activations, cotangent, documents, weight_copy, primary, first_moment, second_moment):
    blocks = lax.axis_size("grp") == 8 and lax.axis_size("rep") == 4
    tiled = primary.shape[0] % 16 == 0 and activations.shape[1] % 16 == 0
    args = (activations, cotangent, documents, weight_copy, primary, first_moment, second_moment)
    return block_body(*args) if blocks and tiled else plain_body(*args)


def solution(mesh):
    in_specs = (
        P(("grp", "rep"), None, None),
        P(("grp", "rep"), None, None),
        P(("grp", "rep"), None),
        P("grp", None),
        P(("grp", "rep"), None),
        P(("grp", "rep"), None),
        P(("grp", "rep"), None),
    )
    out_specs = (
        P(("grp", "rep"), None),
        P(("grp", "rep"), None),
        P(("grp", "rep"), None),
        P("grp", None),
    )
    return jax.shard_map(chosen_body, mesh=mesh, in_specs=in_specs, out_specs=out_specs, check_vma=False)
```

```python
import functools
import math

import jax
import jax.numpy as jnp
from jax import lax
from jax.experimental import pallas as pl
from jax.experimental.pallas import tpu as pltpu
from jax.sharding import PartitionSpec as P

BETA_FIRST = 0.9
BETA_SECOND = 0.95
LEARN_RATE = 6e-05
DECAY_RATE = 0.1
EPSILON = 1e-08
STEP_COUNT = 10.0

AXES = ("grp", "rep")
MIB = 1024 * 1024
FAR = (2, 3)
NEAR = (1, 0)


def adam(gradient, primary, first_moment, second_moment):
    first_new = BETA_FIRST * first_moment + (1.0 - BETA_FIRST) * gradient
    second_new = BETA_SECOND * second_moment + (1.0 - BETA_SECOND) * gradient * gradient
    correct_first = 1.0 - BETA_FIRST**STEP_COUNT
    correct_second = 1.0 - BETA_SECOND**STEP_COUNT
    update = first_new / correct_first / (jnp.sqrt(second_new / correct_second) + EPSILON)
    primary_new = primary - LEARN_RATE * (update + DECAY_RATE * primary)
    return primary_new, first_new, second_new


def plain_body(activations, cotangent, documents, weight_copy, primary, first_moment, second_moment):
    features = activations[0]
    cotan_rows = cotangent[0]
    doc_row = documents[0]
    head = weight_copy.shape[1] // 4
    token_count = features.shape[0]
    grad_scale = 1.0 / math.sqrt(lax.axis_size("grp") * lax.axis_size("rep") * token_count)
    scale_value = 1.0 / math.sqrt(head)
    dot = functools.partial(jnp.dot, preferred_element_type=jnp.float32)
    weights = lax.all_gather(weight_copy, "grp", axis=0, tiled=True)
    projected = dot(features, weights[:, : 3 * head]).astype(jnp.bfloat16)
    back_context = dot(cotan_rows, weights[:, 3 * head :]).astype(jnp.bfloat16)
    queries, key_rows, value_rows = jnp.split(projected, 3, axis=1)
    scores = dot(queries, key_rows.T) * scale_value
    position = jnp.arange(token_count, dtype=jnp.int32)
    allowed = (position[None, :] <= position[:, None]) & (doc_row[None, :] == doc_row[:, None])
    exp_scores = jnp.where(allowed, jnp.exp(jnp.where(allowed, scores, 0.0)), 0.0)
    attention = exp_scores / jnp.sum(exp_scores, axis=1, keepdims=True)
    attention_low = attention.astype(jnp.bfloat16)
    context = dot(attention_low, value_rows).astype(jnp.bfloat16)
    back_attention = dot(back_context, value_rows.T)
    back_values = dot(attention_low.T, back_context).astype(jnp.bfloat16)
    inner_sum = jnp.sum(attention * back_attention, axis=1, keepdims=True)
    back_scores = (attention * (back_attention - inner_sum) * scale_value).astype(jnp.bfloat16)
    back_queries = dot(back_scores, key_rows).astype(jnp.bfloat16)
    back_keys = dot(back_scores.T, queries).astype(jnp.bfloat16)
    back_projected = jnp.concatenate([back_queries, back_keys, back_values], axis=1)
    term = jnp.concatenate([dot(features.T, back_projected), dot(cotan_rows.T, context)], axis=1)
    term = (term * grad_scale).astype(jnp.bfloat16)
    partial_sum = lax.psum_scatter(term, "grp", scatter_dimension=0, tiled=True)
    gradient = lax.psum_scatter(partial_sum, "rep", scatter_dimension=0, tiled=True)
    primary_new, first_new, second_new = adam(
        gradient.astype(jnp.float32), primary, first_moment, second_moment
    )
    copy_new = lax.all_gather(primary_new.astype(jnp.bfloat16), "rep", axis=0, tiled=True)
    return primary_new, first_new, second_new, copy_new


def hop(value, kz, kx, ky, kc):
    offset = (kz * 2 + kx) * 4 + ky * 2 + kc
    return lax.ppermute(value, AXES, [(i, i ^ offset) for i in range(32)])


def join(*parts):
    return jnp.concatenate(parts, axis=0)


def block_start(kz, kx, ky, kc, rows):
    me = lax.axis_index("grp") * 4 + lax.axis_index("rep")
    offset = (kz * 2 + kx) * 4 + ky * 2 + kc
    return pl.multiple_of(lax.bitwise_xor(me, jnp.int32(offset)) * rows, rows)


def chip_start(kz, kx, ky, rows):
    me = lax.axis_index("grp") * 2 + lax.axis_index("rep") // 2
    offset = (kz * 2 + kx) * 2 + ky
    return pl.multiple_of(lax.bitwise_xor(me, jnp.int32(offset)) * (2 * rows), 2 * rows)


def fdot(a, b, dims):
    return lax.dot_general(a, b, (dims, ((), ())), preferred_element_type=jnp.float32)


MM = ((1,), (0,))
MT = ((1,), (1,))
TM = ((0,), (0,))


def project(pieces, places, acts, cots, weights, rows, head):
    chips = []
    core = lax.axis_index("rep") % 2
    for piece, place in zip(pieces, places):
        if place[0] is None:
            for ky in (0, 1):
                chip = (0, 0, ky)
                chips.append(chip)
                offset = (chips.index(chip)) * 2 * rows
                start = pl.multiple_of(chip_start(*chip, rows) % (4 * rows), 2 * rows)
                weights[offset : offset + 2 * rows, :] = piece[pl.ds(start, 2 * rows), :]
            continue
        for index, (*chip, kc) in enumerate(place):
            chip = tuple(chip)
            if chip not in chips:
                chips.append(chip)
            offset = chips.index(chip) * 2 * rows + lax.bitwise_xor(core, jnp.int32(kc)) * rows
            weights[pl.ds(pl.multiple_of(offset, rows), rows), :] = piece[index * rows : (index + 1) * rows, :]
    front = back = 0.0
    for index, chip in enumerate(chips):
        columns = pl.ds(chip_start(*chip, rows), 2 * rows)
        block = weights[index * 2 * rows : (index + 1) * 2 * rows, :]
        front += fdot(acts[:, columns], block[:, : 3 * head], MM)
        back += fdot(cots[:, columns], block[:, 3 * head :], MM)
    return front, back


def turn_kernel(step, source, target):
    for start in range(0, source.shape[1], step):
        target[start : start + step, :] = source[:, start : start + step].T


def early_kernel(places, rows, head, *refs):
    count = len(places)
    acts, cots, front, back, weights = refs[count:]
    front[...], back[...] = project(refs[:count], places, acts, cots, weights, rows, head)


def attend_kernel(places, rows, head, grad_scale, *refs):
    count = len(places)
    acts, cots, docs, acts_t, cots_t, front_ref, back_ref = refs[count : count + 7]
    far_ref, left_ref, right_ref, weights = refs[count + 7 :]
    front, back = project(refs[:count], places, acts, cots, weights, rows, head)
    projected = (front_ref[...] + front).astype(jnp.bfloat16)
    back_context = (back_ref[...] + back).astype(jnp.bfloat16)
    queries = projected[:, :head]
    key_rows = projected[:, head : 2 * head]
    value_rows = projected[:, 2 * head :]
    scale_value = 1.0 / math.sqrt(head)
    scores = fdot(queries, key_rows, MT) * scale_value
    tokens = scores.shape[0]
    here = lax.broadcasted_iota(jnp.int32, (tokens, tokens), 0)
    there = lax.broadcasted_iota(jnp.int32, (tokens, tokens), 1)
    document = jnp.broadcast_to(docs[...], (tokens, tokens))
    allowed = (there <= here) & (document == document.T)
    exp_scores = jnp.where(allowed, jnp.exp(jnp.where(allowed, scores, 0.0)), 0.0)
    attention = exp_scores / jnp.sum(exp_scores, axis=1, keepdims=True)
    attention_low = attention.astype(jnp.bfloat16)
    context = fdot(attention_low, value_rows, MM).astype(jnp.bfloat16)
    back_attention = fdot(back_context, value_rows, MT)
    back_values = fdot(attention_low, back_context, TM).astype(jnp.bfloat16)
    inner_sum = jnp.sum(attention * back_attention, axis=1, keepdims=True)
    back_scores = (attention * (back_attention - inner_sum) * scale_value).astype(jnp.bfloat16)
    back_queries = fdot(back_scores, key_rows, MM).astype(jnp.bfloat16)
    back_keys = fdot(back_scores, queries, TM).astype(jnp.bfloat16)
    none = jnp.zeros((tokens, head), jnp.bfloat16)
    left = jnp.concatenate([back_queries, back_keys, back_values, none], axis=1)
    right = jnp.concatenate([none, none, none, context], axis=1)
    left_ref[...] = left
    right_ref[...] = right
    write_terms(acts_t, cots_t, left, right, far_ref, FAR, 1, rows, grad_scale)


def write_terms(acts_t, cots_t, left, right, out_ref, kzs, kc, rows, grad_scale):
    for index, (kz, kx, ky) in enumerate((kz, kx, ky) for kz in kzs for kx in (0, 1) for ky in (0, 1)):
        start = block_start(kz, kx, ky, kc, rows)
        term = fdot(acts_t[pl.ds(start, rows), :], left, MM)
        term += fdot(cots_t[pl.ds(start, rows), :], right, MM)
        out_ref[index * rows : (index + 1) * rows, :] = (term * grad_scale).astype(out_ref.dtype)


def terms_kernel(kzs, kc, rows, grad_scale, acts_t, cots_t, left_ref, right_ref, out_ref):
    write_terms(acts_t, cots_t, left_ref[...], right_ref[...], out_ref, kzs, kc, rows, grad_scale)


def vmem(count):
    return [pl.BlockSpec(memory_space=pltpu.VMEM)] * count


def kernel_call(body, outs, name, args, scratch=(), flops=0, limit=16):
    return pl.pallas_call(
        body,
        out_shape=outs,
        in_specs=vmem(len(args)),
        out_specs=vmem(len(outs)),
        scratch_shapes=scratch,
        name=name,
        compiler_params=pltpu.CompilerParams(vmem_limit_bytes=limit * MIB),
        cost_estimate=pl.CostEstimate(flops=flops, bytes_accessed=4 * MIB, transcendentals=0),
    )(*args)


def gather(weight_copy, rows, first, second):
    rep = lax.axis_index("rep")
    own = lax.dynamic_slice_in_dim(weight_copy, rep * rows, rows, 0)
    half = lax.dynamic_slice_in_dim(weight_copy, jnp.bitwise_xor(rep, 2) * rows, rows, 0)
    both = join(own, half)
    z2 = hop(own, 2, 0, 0, 0)
    x0 = hop(both, 0, 1, 0, 0)
    z2, first = lax.optimization_barrier((z2, first))
    z1 = hop(both, 1, 0, 0, 0)
    z3 = hop(z2, 1, 0, 0, 0)
    x2 = hop(z2, 0, 1, 0, 0)
    z3, x0, x2 = lax.optimization_barrier((z3, x0, x2))
    x3 = hop(z3, 0, 1, 0, 0)
    ya = hop(join(z2, z3, x2), 0, 0, 1, 0)
    zx = hop(x0, 1, 0, 0, 0)
    yb = hop(x3, 0, 0, 1, 0)
    yb, second = lax.optimization_barrier((yb, second))

    def both_cores(arrays, places):
        other = hop(join(*arrays), 0, 0, 0, 1)
        pieces = [(array, [(*at, 0) for at in place]) for array, place in zip(arrays, places)]
        return pieces + [(other, [(*at, 1) for place in places for at in place])]

    early = both_cores(
        (x0, z1, z2, z3, x2),
        ([(0, 1, 0), (0, 1, 1)], [(1, 0, 0), (1, 0, 1)], [(2, 0, 0)], [(3, 0, 0)], [(2, 1, 0)]),
    )
    late = both_cores(
        (x3, zx, ya, yb),
        ([(3, 1, 0)], [(1, 1, 0), (1, 1, 1)], [(2, 0, 1), (3, 0, 1), (2, 1, 1)], [(3, 1, 1)]),
    )
    return [(weight_copy, [None]), *early], late, first, second


def plane_sum(mine, received, kzs, rows):
    def block(kz, kx, ky):
        start = ((kzs.index(kz) * 2 + kx) * 2 + ky) * rows
        return mine[start : start + rows] + received[start : start + rows].astype(jnp.float32)

    totals = [block(kz, 0, 0) for kz in kzs]
    for kx, ky in ((1, 1), (1, 0), (0, 1)):
        came = hop(join(*[block(kz, kx, ky).astype(jnp.bfloat16) for kz in kzs]), 0, kx, ky, 0)
        for index in range(len(kzs)):
            totals[index] += came[index * rows : (index + 1) * rows].astype(jnp.float32)
    return totals


def block_body(activations, cotangent, documents, weight_copy, primary, first_moment, second_moment):
    acts, cots = activations[0], cotangent[0]
    tokens, depth = acts.shape
    columns = weight_copy.shape[1]
    rows = primary.shape[0]
    head = columns // 4
    grad_scale = 1.0 / math.sqrt(32 * tokens)
    bfloat = functools.partial(jax.ShapeDtypeStruct, dtype=jnp.bfloat16)
    float32 = functools.partial(jax.ShapeDtypeStruct, dtype=jnp.float32)
    flops = 4 * tokens * depth * columns

    acts_t, cots_t = [
        kernel_call(
            functools.partial(turn_kernel, 512), [bfloat((depth, tokens))], "turn", (source,), flops=flops // 2
        )[0]
        for source in (acts, cots)
    ]
    early, late, acts_t, cots_t = gather(weight_copy, rows, acts_t, cots_t)
    front, back = kernel_call(
        functools.partial(early_kernel, [place for _, place in early], rows, head),
        [float32((tokens, 3 * head)), float32((tokens, head))],
        "early",
        (*[piece for piece, _ in early], acts, cots),
        scratch=[pltpu.VMEM((24 * rows, columns), jnp.bfloat16)],
        flops=flops,
    )
    far, left, right = kernel_call(
        functools.partial(attend_kernel, [place for _, place in late], rows, head, grad_scale),
        [bfloat((8 * rows, columns))] + [bfloat((tokens, columns))] * 2,
        "attend",
        (*[piece for piece, _ in late], acts, cots, documents, acts_t, cots_t, front, back),
        scratch=[pltpu.VMEM((16 * rows, columns), jnp.bfloat16)],
        flops=flops,
    )

    def terms(kzs, kc, dtype):
        return kernel_call(
            functools.partial(terms_kernel, kzs, kc, rows, grad_scale),
            [dtype((4 * len(kzs) * rows, columns))],
            "terms",
            (acts_t, cots_t, left, right),
            flops=flops * len(kzs) // 8,
        )[0]

    totals = {}
    for kzs, sent in ((FAR, far), (NEAR, terms(NEAR, 1, bfloat))):
        received = hop(sent, 0, 0, 0, 1)
        totals.update(zip(kzs, plane_sum(terms(kzs, 0, float32), received, kzs, rows)))
    gradient = totals[0]
    for kz in (2, 3, 1):
        gradient += hop(totals[kz].astype(jnp.bfloat16), kz, 0, 0, 0).astype(jnp.float32)
    primary_new, first_new, second_new = adam(gradient, primary, first_moment, second_moment)
    copy_new = lax.all_gather(primary_new.astype(jnp.bfloat16), "rep", axis=0, tiled=True)
    return primary_new, first_new, second_new, copy_new


def chosen_body(activations, cotangent, documents, weight_copy, primary, first_moment, second_moment):
    blocks = lax.axis_size("grp") == 8 and lax.axis_size("rep") == 4
    tiled = primary.shape[0] % 16 == 0 and activations.shape[1] % 16 == 0
    args = (activations, cotangent, documents, weight_copy, primary, first_moment, second_moment)
    return block_body(*args) if blocks and tiled else plain_body(*args)


def solution(mesh):
    in_specs = (
        P(("grp", "rep"), None, None),
        P(("grp", "rep"), None, None),
        P(("grp", "rep"), None),
        P("grp", None),
        P(("grp", "rep"), None),
        P(("grp", "rep"), None),
        P(("grp", "rep"), None),
    )
    out_specs = (
        P(("grp", "rep"), None),
        P(("grp", "rep"), None),
        P(("grp", "rep"), None),
        P("grp", None),
    )
    return jax.shard_map(chosen_body, mesh=mesh, in_specs=in_specs, out_specs=out_specs, check_vma=False)
```

```python
import functools
import math

import jax
import jax.numpy as jnp
from jax import lax
from jax.experimental import pallas as pl
from jax.experimental.pallas import tpu as pltpu
from jax.sharding import PartitionSpec as P

BETA_FIRST = 0.9
BETA_SECOND = 0.95
LEARN_RATE = 6e-05
DECAY_RATE = 0.1
EPSILON = 1e-08
STEP_COUNT = 10.0

AXES = ("grp", "rep")
MIB = 1024 * 1024


def adam(gradient, primary, first_moment, second_moment):
    first_new = BETA_FIRST * first_moment + (1.0 - BETA_FIRST) * gradient
    second_new = BETA_SECOND * second_moment + (1.0 - BETA_SECOND) * gradient * gradient
    correct_first = 1.0 - BETA_FIRST**STEP_COUNT
    correct_second = 1.0 - BETA_SECOND**STEP_COUNT
    update = first_new / correct_first / (jnp.sqrt(second_new / correct_second) + EPSILON)
    primary_new = primary - LEARN_RATE * (update + DECAY_RATE * primary)
    return primary_new, first_new, second_new


def plain_body(activations, cotangent, documents, weight_copy, primary, first_moment, second_moment):
    features = activations[0]
    cotan_rows = cotangent[0]
    doc_row = documents[0]
    head = weight_copy.shape[1] // 4
    token_count = features.shape[0]
    grad_scale = 1.0 / math.sqrt(lax.axis_size("grp") * lax.axis_size("rep") * token_count)
    scale_value = 1.0 / math.sqrt(head)
    dot = functools.partial(jnp.dot, preferred_element_type=jnp.float32)
    weights = lax.all_gather(weight_copy, "grp", axis=0, tiled=True)
    projected = dot(features, weights[:, : 3 * head]).astype(jnp.bfloat16)
    back_context = dot(cotan_rows, weights[:, 3 * head :]).astype(jnp.bfloat16)
    queries, key_rows, value_rows = jnp.split(projected, 3, axis=1)
    scores = dot(queries, key_rows.T) * scale_value
    position = jnp.arange(token_count, dtype=jnp.int32)
    allowed = (position[None, :] <= position[:, None]) & (doc_row[None, :] == doc_row[:, None])
    exp_scores = jnp.where(allowed, jnp.exp(jnp.where(allowed, scores, 0.0)), 0.0)
    attention = exp_scores / jnp.sum(exp_scores, axis=1, keepdims=True)
    attention_low = attention.astype(jnp.bfloat16)
    context = dot(attention_low, value_rows).astype(jnp.bfloat16)
    back_attention = dot(back_context, value_rows.T)
    back_values = dot(attention_low.T, back_context).astype(jnp.bfloat16)
    inner_sum = jnp.sum(attention * back_attention, axis=1, keepdims=True)
    back_scores = (attention * (back_attention - inner_sum) * scale_value).astype(jnp.bfloat16)
    back_queries = dot(back_scores, key_rows).astype(jnp.bfloat16)
    back_keys = dot(back_scores.T, queries).astype(jnp.bfloat16)
    back_projected = jnp.concatenate([back_queries, back_keys, back_values], axis=1)
    term = jnp.concatenate([dot(features.T, back_projected), dot(cotan_rows.T, context)], axis=1)
    term = (term * grad_scale).astype(jnp.bfloat16)
    partial_sum = lax.psum_scatter(term, "grp", scatter_dimension=0, tiled=True)
    gradient = lax.psum_scatter(partial_sum, "rep", scatter_dimension=0, tiled=True)
    primary_new, first_new, second_new = adam(
        gradient.astype(jnp.float32), primary, first_moment, second_moment
    )
    copy_new = lax.all_gather(primary_new.astype(jnp.bfloat16), "rep", axis=0, tiled=True)
    return primary_new, first_new, second_new, copy_new


def hop(value, kz, kx, ky, kc):
    offset = (kz * 2 + kx) * 4 + ky * 2 + kc
    return lax.ppermute(value, AXES, [(i, i ^ offset) for i in range(32)])


def join(*parts):
    return jnp.concatenate(parts, axis=0)


def block_start(kz, kx, ky, kc, rows):
    me = lax.axis_index("grp") * 4 + lax.axis_index("rep")
    offset = (kz * 2 + kx) * 4 + ky * 2 + kc
    return pl.multiple_of(lax.bitwise_xor(me, jnp.int32(offset)) * rows, rows)


def chip_start(kz, kx, ky, rows):
    me = lax.axis_index("grp") * 2 + lax.axis_index("rep") // 2
    offset = (kz * 2 + kx) * 2 + ky
    return pl.multiple_of(lax.bitwise_xor(me, jnp.int32(offset)) * (2 * rows), 2 * rows)


def fdot(a, b, dims):
    return lax.dot_general(a, b, (dims, ((), ())), preferred_element_type=jnp.float32)


MM = ((1,), (0,))
MT = ((1,), (1,))
TM = ((0,), (0,))


def project(pieces, places, acts, cots, weights, rows, head):
    chips = []
    core = lax.axis_index("rep") % 2
    for piece, place in zip(pieces, places):
        if place[0] is None:
            for ky in (0, 1):
                chip = (0, 0, ky)
                chips.append(chip)
                offset = (chips.index(chip)) * 2 * rows
                start = pl.multiple_of(chip_start(*chip, rows) % (4 * rows), 2 * rows)
                weights[offset : offset + 2 * rows, :] = piece[pl.ds(start, 2 * rows), :]
            continue
        for index, (*chip, kc) in enumerate(place):
            chip = tuple(chip)
            if chip not in chips:
                chips.append(chip)
            offset = chips.index(chip) * 2 * rows + lax.bitwise_xor(core, jnp.int32(kc)) * rows
            weights[pl.ds(pl.multiple_of(offset, rows), rows), :] = piece[index * rows : (index + 1) * rows, :]
    front = back = 0.0
    for index, chip in enumerate(chips):
        columns = pl.ds(chip_start(*chip, rows), 2 * rows)
        block = weights[index * 2 * rows : (index + 1) * 2 * rows, :]
        front += fdot(acts[:, columns], block[:, : 3 * head], MM)
        back += fdot(cots[:, columns], block[:, 3 * head :], MM)
    return front, back


def turn_kernel(step, source, target):
    for start in range(0, source.shape[1], step):
        target[start : start + step, :] = source[:, start : start + step].T


def early_kernel(places, rows, head, *refs):
    count = len(places)
    acts, cots, front, back, weights = refs[count:]
    front[...], back[...] = project(refs[:count], places, acts, cots, weights, rows, head)


def attend_kernel(places, blocks, rows, head, grad_scale, *refs):
    count = len(places)
    acts, cots, docs, acts_t, cots_t, front_ref, back_ref = refs[count : count + 7]
    sent_ref, left_ref, right_ref, weights = refs[count + 7 :]
    front, back = project(refs[:count], places, acts, cots, weights, rows, head)
    projected = (front_ref[...] + front).astype(jnp.bfloat16)
    back_context = (back_ref[...] + back).astype(jnp.bfloat16)
    queries = projected[:, :head]
    key_rows = projected[:, head : 2 * head]
    value_rows = projected[:, 2 * head :]
    scale_value = 1.0 / math.sqrt(head)
    scores = fdot(queries, key_rows, MT) * scale_value
    tokens = scores.shape[0]
    here = lax.broadcasted_iota(jnp.int32, (tokens, tokens), 0)
    there = lax.broadcasted_iota(jnp.int32, (tokens, tokens), 1)
    document = jnp.broadcast_to(docs[...], (tokens, tokens))
    allowed = (there <= here) & (document == document.T)
    exp_scores = jnp.where(allowed, jnp.exp(jnp.where(allowed, scores, 0.0)), 0.0)
    attention = exp_scores / jnp.sum(exp_scores, axis=1, keepdims=True)
    attention_low = attention.astype(jnp.bfloat16)
    context = fdot(attention_low, value_rows, MM).astype(jnp.bfloat16)
    back_attention = fdot(back_context, value_rows, MT)
    back_values = fdot(attention_low, back_context, TM).astype(jnp.bfloat16)
    inner_sum = jnp.sum(attention * back_attention, axis=1, keepdims=True)
    back_scores = (attention * (back_attention - inner_sum) * scale_value).astype(jnp.bfloat16)
    back_queries = fdot(back_scores, key_rows, MM).astype(jnp.bfloat16)
    back_keys = fdot(back_scores, queries, TM).astype(jnp.bfloat16)
    none = jnp.zeros((tokens, head), jnp.bfloat16)
    left = jnp.concatenate([back_queries, back_keys, back_values, none], axis=1)
    right = jnp.concatenate([none, none, none, context], axis=1)
    left_ref[...] = left
    right_ref[...] = right
    write_terms(acts_t, cots_t, left, right, sent_ref, blocks, 1, rows, grad_scale)


def write_terms(acts_t, cots_t, left, right, out_ref, blocks, kc, rows, grad_scale):
    for index, block in enumerate(blocks):
        start = block_start(*block, kc, rows)
        term = fdot(acts_t[pl.ds(start, rows), :], left, MM)
        term += fdot(cots_t[pl.ds(start, rows), :], right, MM)
        out_ref[index * rows : (index + 1) * rows, :] = (term * grad_scale).astype(out_ref.dtype)


def terms_kernel(blocks, kc, rows, grad_scale, acts_t, cots_t, left_ref, right_ref, out_ref):
    write_terms(acts_t, cots_t, left_ref[...], right_ref[...], out_ref, blocks, kc, rows, grad_scale)


def vmem(count):
    return [pl.BlockSpec(memory_space=pltpu.VMEM)] * count


def kernel_call(body, outs, name, args, scratch=(), flops=0, limit=16):
    return pl.pallas_call(
        body,
        out_shape=outs,
        in_specs=vmem(len(args)),
        out_specs=vmem(len(outs)),
        scratch_shapes=scratch,
        name=name,
        compiler_params=pltpu.CompilerParams(vmem_limit_bytes=limit * MIB),
        cost_estimate=pl.CostEstimate(flops=flops, bytes_accessed=4 * MIB, transcendentals=0),
    )(*args)


def gather(weight_copy, rows, first, second):
    rep = lax.axis_index("rep")
    own = lax.dynamic_slice_in_dim(weight_copy, rep * rows, rows, 0)
    half = lax.dynamic_slice_in_dim(weight_copy, jnp.bitwise_xor(rep, 2) * rows, rows, 0)
    both = join(own, half)
    z2 = hop(own, 2, 0, 0, 0)
    x0 = hop(both, 0, 1, 0, 0)
    z2, first = lax.optimization_barrier((z2, first))
    z1 = hop(both, 1, 0, 0, 0)
    z3 = hop(z2, 1, 0, 0, 0)
    x2 = hop(z2, 0, 1, 0, 0)
    z3, x0, x2 = lax.optimization_barrier((z3, x0, x2))
    x3 = hop(z3, 0, 1, 0, 0)
    ya = hop(join(z2, z3, x2), 0, 0, 1, 0)
    zx = hop(x0, 1, 0, 0, 0)
    yb = hop(x3, 0, 0, 1, 0)
    yb, second = lax.optimization_barrier((yb, second))

    def both_cores(arrays, places):
        other = hop(join(*arrays), 0, 0, 0, 1)
        pieces = [(array, [(*at, 0) for at in place]) for array, place in zip(arrays, places)]
        return pieces + [(other, [(*at, 1) for place in places for at in place])]

    early = both_cores(
        (x0, z1, z2, z3, x2),
        ([(0, 1, 0), (0, 1, 1)], [(1, 0, 0), (1, 0, 1)], [(2, 0, 0)], [(3, 0, 0)], [(2, 1, 0)]),
    )
    late = both_cores(
        (x3, zx, ya, yb),
        ([(3, 1, 0)], [(1, 1, 0), (1, 1, 1)], [(2, 0, 1), (3, 0, 1), (2, 1, 1)], [(3, 1, 1)]),
    )
    return [(weight_copy, [None]), *early], late, first, second


SIDES = ((1, 1), (1, 0), (0, 1))


def cut(array, count):
    size = array.shape[0] // count
    return [array[index * size : (index + 1) * size] for index in range(count)]


def add(*parts):
    return sum(part.astype(jnp.float32) for part in parts)


def low(array):
    return array.astype(jnp.bfloat16)


def block_body(activations, cotangent, documents, weight_copy, primary, first_moment, second_moment):
    acts, cots = activations[0], cotangent[0]
    tokens, depth = acts.shape
    columns = weight_copy.shape[1]
    rows = primary.shape[0]
    head = columns // 4
    grad_scale = 1.0 / math.sqrt(32 * tokens)
    bfloat = functools.partial(jax.ShapeDtypeStruct, dtype=jnp.bfloat16)
    float32 = functools.partial(jax.ShapeDtypeStruct, dtype=jnp.float32)
    flops = 4 * tokens * depth * columns

    acts_t, cots_t = [
        kernel_call(
            functools.partial(turn_kernel, 512), [bfloat((depth, tokens))], "turn", (source,), flops=flops // 2
        )[0]
        for source in (acts, cots)
    ]
    early, late, acts_t, cots_t = gather(weight_copy, rows, acts_t, cots_t)
    front, back = kernel_call(
        functools.partial(early_kernel, [place for _, place in early], rows, head),
        [float32((tokens, 3 * head)), float32((tokens, head))],
        "early",
        (*[piece for piece, _ in early], acts, cots),
        scratch=[pltpu.VMEM((24 * rows, columns), jnp.bfloat16)],
        flops=flops,
    )
    far = [(kz, kx, ky) for kx, ky in (*SIDES, (0, 0)) for kz in (2, 3)]
    near = [(kz, kx, ky) for kz in (1, 0) for kx, ky in (*SIDES, (0, 0))]
    sent, left, right = kernel_call(
        functools.partial(attend_kernel, [place for _, place in late], far[:2], rows, head, grad_scale),
        [bfloat((2 * rows, columns))] + [bfloat((tokens, columns))] * 2,
        "attend",
        (*[piece for piece, _ in late], acts, cots, documents, acts_t, cots_t, front, back),
        scratch=[pltpu.VMEM((16 * rows, columns), jnp.bfloat16)],
        flops=flops,
    )

    def terms(blocks, kc, dtype):
        return kernel_call(
            functools.partial(terms_kernel, blocks, kc, rows, grad_scale),
            [dtype((len(blocks) * rows, columns))],
            "terms",
            (acts_t, cots_t, left, right),
            flops=flops * len(blocks) // 32,
        )[0]

    def other_core(value):
        return hop(value, 0, 0, 0, 1)

    sent = other_core(sent)
    rest = other_core(terms(far[2:], 1, bfloat))
    near_other = other_core(terms(near, 1, bfloat))
    mine = terms(far, 0, float32)
    diagonal = add(mine[: 2 * rows], sent)
    along_x, along_y, total = cut(add(mine[2 * rows :], rest), 3)
    total = add(total, *[hop(low(part), 0, *side, 0) for part, side in zip((diagonal, along_x, along_y), SIDES)])
    total_2, total_3 = cut(total, 2)
    one, zero = cut(add(terms(near, 0, float32), near_other), 2)
    *parts, gradient = cut(add(zero, hop(low(one), 1, 0, 0, 0)), 4)
    arrived = [hop(low(part), 0, *side, 0) for part, side in zip(parts, SIDES)]
    arrived += [hop(low(total_2), 2, 0, 0, 0), hop(low(total_3), 3, 0, 0, 0)]
    gradient = add(gradient, *arrived)
    primary_new, first_new, second_new = adam(gradient, primary, first_moment, second_moment)
    copy_new = lax.all_gather(primary_new.astype(jnp.bfloat16), "rep", axis=0, tiled=True)
    return primary_new, first_new, second_new, copy_new


def chosen_body(activations, cotangent, documents, weight_copy, primary, first_moment, second_moment):
    blocks = lax.axis_size("grp") == 8 and lax.axis_size("rep") == 4
    tiled = primary.shape[0] % 16 == 0 and activations.shape[1] % 16 == 0
    args = (activations, cotangent, documents, weight_copy, primary, first_moment, second_moment)
    return block_body(*args) if blocks and tiled else plain_body(*args)


def solution(mesh):
    in_specs = (
        P(("grp", "rep"), None, None),
        P(("grp", "rep"), None, None),
        P(("grp", "rep"), None),
        P("grp", None),
        P(("grp", "rep"), None),
        P(("grp", "rep"), None),
        P(("grp", "rep"), None),
    )
    out_specs = (
        P(("grp", "rep"), None),
        P(("grp", "rep"), None),
        P(("grp", "rep"), None),
        P("grp", None),
    )
    return jax.shard_map(chosen_body, mesh=mesh, in_specs=in_specs, out_specs=out_specs, check_vma=False)
```

```python
import functools
import math

import jax
import jax.numpy as jnp
from jax import lax
from jax.experimental import pallas as pl
from jax.experimental.pallas import tpu as pltpu
from jax.sharding import PartitionSpec as P

BETA_FIRST = 0.9
BETA_SECOND = 0.95
LEARN_RATE = 6e-05
DECAY_RATE = 0.1
EPSILON = 1e-08
STEP_COUNT = 10.0

AXES = ("grp", "rep")
MIB = 1024 * 1024


def adam(gradient, primary, first_moment, second_moment):
    first_new = BETA_FIRST * first_moment + (1.0 - BETA_FIRST) * gradient
    second_new = BETA_SECOND * second_moment + (1.0 - BETA_SECOND) * gradient * gradient
    correct_first = 1.0 - BETA_FIRST**STEP_COUNT
    correct_second = 1.0 - BETA_SECOND**STEP_COUNT
    update = first_new / correct_first / (jnp.sqrt(second_new / correct_second) + EPSILON)
    primary_new = primary - LEARN_RATE * (update + DECAY_RATE * primary)
    return primary_new, first_new, second_new


def plain_body(activations, cotangent, documents, weight_copy, primary, first_moment, second_moment):
    features = activations[0]
    cotan_rows = cotangent[0]
    doc_row = documents[0]
    head = weight_copy.shape[1] // 4
    token_count = features.shape[0]
    grad_scale = 1.0 / math.sqrt(lax.axis_size("grp") * lax.axis_size("rep") * token_count)
    scale_value = 1.0 / math.sqrt(head)
    dot = functools.partial(jnp.dot, preferred_element_type=jnp.float32)
    weights = lax.all_gather(weight_copy, "grp", axis=0, tiled=True)
    projected = dot(features, weights[:, : 3 * head]).astype(jnp.bfloat16)
    back_context = dot(cotan_rows, weights[:, 3 * head :]).astype(jnp.bfloat16)
    queries, key_rows, value_rows = jnp.split(projected, 3, axis=1)
    scores = dot(queries, key_rows.T) * scale_value
    position = jnp.arange(token_count, dtype=jnp.int32)
    allowed = (position[None, :] <= position[:, None]) & (doc_row[None, :] == doc_row[:, None])
    exp_scores = jnp.where(allowed, jnp.exp(jnp.where(allowed, scores, 0.0)), 0.0)
    attention = exp_scores / jnp.sum(exp_scores, axis=1, keepdims=True)
    attention_low = attention.astype(jnp.bfloat16)
    context = dot(attention_low, value_rows).astype(jnp.bfloat16)
    back_attention = dot(back_context, value_rows.T)
    back_values = dot(attention_low.T, back_context).astype(jnp.bfloat16)
    inner_sum = jnp.sum(attention * back_attention, axis=1, keepdims=True)
    back_scores = (attention * (back_attention - inner_sum) * scale_value).astype(jnp.bfloat16)
    back_queries = dot(back_scores, key_rows).astype(jnp.bfloat16)
    back_keys = dot(back_scores.T, queries).astype(jnp.bfloat16)
    back_projected = jnp.concatenate([back_queries, back_keys, back_values], axis=1)
    term = jnp.concatenate([dot(features.T, back_projected), dot(cotan_rows.T, context)], axis=1)
    term = (term * grad_scale).astype(jnp.bfloat16)
    partial_sum = lax.psum_scatter(term, "grp", scatter_dimension=0, tiled=True)
    gradient = lax.psum_scatter(partial_sum, "rep", scatter_dimension=0, tiled=True)
    primary_new, first_new, second_new = adam(
        gradient.astype(jnp.float32), primary, first_moment, second_moment
    )
    copy_new = lax.all_gather(primary_new.astype(jnp.bfloat16), "rep", axis=0, tiled=True)
    return primary_new, first_new, second_new, copy_new


def hop(value, kz, kx, ky, kc):
    offset = (kz * 2 + kx) * 4 + ky * 2 + kc
    return lax.ppermute(value, AXES, [(i, i ^ offset) for i in range(32)])


def join(*parts):
    return jnp.concatenate(parts, axis=0)


def block_start(kz, kx, ky, kc, rows):
    me = lax.axis_index("grp") * 4 + lax.axis_index("rep")
    offset = (kz * 2 + kx) * 4 + ky * 2 + kc
    return pl.multiple_of(lax.bitwise_xor(me, jnp.int32(offset)) * rows, rows)


def chip_start(kz, kx, ky, rows):
    me = lax.axis_index("grp") * 2 + lax.axis_index("rep") // 2
    offset = (kz * 2 + kx) * 2 + ky
    return pl.multiple_of(lax.bitwise_xor(me, jnp.int32(offset)) * (2 * rows), 2 * rows)


def fdot(a, b, dims):
    return lax.dot_general(a, b, (dims, ((), ())), preferred_element_type=jnp.float32)


MM = ((1,), (0,))
MT = ((1,), (1,))
TM = ((0,), (0,))


def project(pieces, places, acts, cots, weights, rows, head):
    chips = []
    core = lax.axis_index("rep") % 2
    for piece, place in zip(pieces, places):
        if place[0] is None:
            for ky in (0, 1):
                chip = (0, 0, ky)
                chips.append(chip)
                offset = (chips.index(chip)) * 2 * rows
                start = pl.multiple_of(chip_start(*chip, rows) % (4 * rows), 2 * rows)
                weights[offset : offset + 2 * rows, :] = piece[pl.ds(start, 2 * rows), :]
            continue
        for index, (*chip, kc) in enumerate(place):
            chip = tuple(chip)
            if chip not in chips:
                chips.append(chip)
            offset = chips.index(chip) * 2 * rows + lax.bitwise_xor(core, jnp.int32(kc)) * rows
            weights[pl.ds(pl.multiple_of(offset, rows), rows), :] = piece[index * rows : (index + 1) * rows, :]
    front = back = 0.0
    for index, chip in enumerate(chips):
        columns = pl.ds(chip_start(*chip, rows), 2 * rows)
        block = weights[index * 2 * rows : (index + 1) * 2 * rows, :]
        front += fdot(acts[:, columns], block[:, : 3 * head], MM)
        back += fdot(cots[:, columns], block[:, 3 * head :], MM)
    return front, back


def turn_kernel(step, source, target):
    for start in range(0, source.shape[1], step):
        target[start : start + step, :] = source[:, start : start + step].T


def early_kernel(places, rows, head, *refs):
    count = len(places)
    acts, cots, front, back, weights = refs[count:]
    front[...], back[...] = project(refs[:count], places, acts, cots, weights, rows, head)


def attend_kernel(places, blocks, rows, head, grad_scale, *refs):
    count = len(places)
    acts, cots, docs, acts_t, cots_t, front_ref, back_ref = refs[count : count + 7]
    sent_ref, left_ref, right_ref, weights = refs[count + 7 :]
    front, back = project(refs[:count], places, acts, cots, weights, rows, head)
    projected = (front_ref[...] + front).astype(jnp.bfloat16)
    back_context = (back_ref[...] + back).astype(jnp.bfloat16)
    queries = projected[:, :head]
    key_rows = projected[:, head : 2 * head]
    value_rows = projected[:, 2 * head :]
    scale_value = 1.0 / math.sqrt(head)
    scores = fdot(queries, key_rows, MT) * scale_value
    tokens = scores.shape[0]
    here = lax.broadcasted_iota(jnp.int32, (tokens, tokens), 0)
    there = lax.broadcasted_iota(jnp.int32, (tokens, tokens), 1)
    document = jnp.broadcast_to(docs[...], (tokens, tokens))
    allowed = (there <= here) & (document == document.T)
    exp_scores = jnp.where(allowed, jnp.exp(jnp.where(allowed, scores, 0.0)), 0.0)
    attention = exp_scores / jnp.sum(exp_scores, axis=1, keepdims=True)
    attention_low = attention.astype(jnp.bfloat16)
    context = fdot(attention_low, value_rows, MM).astype(jnp.bfloat16)
    back_attention = fdot(back_context, value_rows, MT)
    back_values = fdot(attention_low, back_context, TM).astype(jnp.bfloat16)
    inner_sum = jnp.sum(attention * back_attention, axis=1, keepdims=True)
    back_scores = (attention * (back_attention - inner_sum) * scale_value).astype(jnp.bfloat16)
    back_queries = fdot(back_scores, key_rows, MM).astype(jnp.bfloat16)
    back_keys = fdot(back_scores, queries, TM).astype(jnp.bfloat16)
    none = jnp.zeros((tokens, head), jnp.bfloat16)
    left = jnp.concatenate([back_queries, back_keys, back_values, none], axis=1)
    right = jnp.concatenate([none, none, none, context], axis=1)
    left_ref[...] = left
    right_ref[...] = right
    write_terms(acts_t, cots_t, left, right, sent_ref, blocks, 1, rows, grad_scale)


def write_terms(acts_t, cots_t, left, right, out_ref, blocks, kc, rows, grad_scale):
    for index, block in enumerate(blocks):
        start = block_start(*block, kc, rows)
        term = fdot(acts_t[pl.ds(start, rows), :], left, MM)
        term += fdot(cots_t[pl.ds(start, rows), :], right, MM)
        out_ref[index * rows : (index + 1) * rows, :] = (term * grad_scale).astype(out_ref.dtype)


def terms_kernel(blocks, kc, rows, grad_scale, acts_t, cots_t, left_ref, right_ref, out_ref):
    write_terms(acts_t, cots_t, left_ref[...], right_ref[...], out_ref, blocks, kc, rows, grad_scale)


def vmem(count):
    return [pl.BlockSpec(memory_space=pltpu.VMEM)] * count


def kernel_call(body, outs, name, args, scratch=(), flops=0, limit=16):
    return pl.pallas_call(
        body,
        out_shape=outs,
        in_specs=vmem(len(args)),
        out_specs=vmem(len(outs)),
        scratch_shapes=scratch,
        name=name,
        compiler_params=pltpu.CompilerParams(vmem_limit_bytes=limit * MIB),
        cost_estimate=pl.CostEstimate(flops=flops, bytes_accessed=4 * MIB, transcendentals=0),
    )(*args)


def gather(weight_copy, rows, first, second):
    rep = lax.axis_index("rep")
    own = lax.dynamic_slice_in_dim(weight_copy, rep * rows, rows, 0)
    half = lax.dynamic_slice_in_dim(weight_copy, jnp.bitwise_xor(rep, 2) * rows, rows, 0)
    both = join(own, half)
    z2 = hop(own, 2, 0, 0, 0)
    x0 = hop(both, 0, 1, 0, 0)
    z2, first = lax.optimization_barrier((z2, first))
    z1 = hop(both, 1, 0, 0, 0)
    z3 = hop(z2, 1, 0, 0, 0)
    x2 = hop(z2, 0, 1, 0, 0)
    y2 = hop(z2, 0, 0, 1, 0)

    z3, x0, x2 = lax.optimization_barrier((z3, x0, x2))
    x3 = hop(z3, 0, 1, 0, 0)
    ya = hop(join(z3, x2), 0, 0, 1, 0)
    zx = hop(z1, 0, 1, 0, 0)
    yb = hop(x3, 0, 0, 1, 0)
    yb, second = lax.optimization_barrier((yb, second))

    def both_cores(arrays, places):
        other = hop(join(*arrays), 0, 0, 0, 1)
        pieces = [(array, [(*at, 0) for at in place]) for array, place in zip(arrays, places)]
        return pieces + [(other, [(*at, 1) for place in places for at in place])]

    early = both_cores((x0, z2, z3, x2, y2, x3,), ([(0, 1, 0), (0, 1, 1)], [(2, 0, 0)], [(3, 0, 0)], [(2, 1, 0)], [(2, 0, 1)], [(3, 1, 0)],))
    late = both_cores((z1, zx, ya, yb,), ([(1, 0, 0), (1, 0, 1)], [(1, 1, 0), (1, 1, 1)], [(3, 0, 1), (2, 1, 1)], [(3, 1, 1)],))
    return [(weight_copy, [None]), *early], late, first, second


SIDES = ((1, 1), (0, 1), (1, 0))


def cut(array, count):
    size = array.shape[0] // count
    return [array[index * size : (index + 1) * size] for index in range(count)]


def add(*parts):
    return sum(part.astype(jnp.float32) for part in parts)


def low(array):
    return array.astype(jnp.bfloat16)


def block_body(activations, cotangent, documents, weight_copy, primary, first_moment, second_moment):
    acts, cots = activations[0], cotangent[0]
    tokens, depth = acts.shape
    columns = weight_copy.shape[1]
    rows = primary.shape[0]
    head = columns // 4
    grad_scale = 1.0 / math.sqrt(32 * tokens)
    bfloat = functools.partial(jax.ShapeDtypeStruct, dtype=jnp.bfloat16)
    float32 = functools.partial(jax.ShapeDtypeStruct, dtype=jnp.float32)
    flops = 4 * tokens * depth * columns

    acts_t, cots_t = [
        kernel_call(
            functools.partial(turn_kernel, 512), [bfloat((depth, tokens))], "turn", (source,), flops=flops // 2
        )[0]
        for source in (acts, cots)
    ]
    early, late, acts_t, cots_t = gather(weight_copy, rows, acts_t, cots_t)
    front, back = kernel_call(
        functools.partial(early_kernel, [place for _, place in early], rows, head),
        [float32((tokens, 3 * head)), float32((tokens, head))],
        "early",
        (*[piece for piece, _ in early], acts, cots),
        scratch=[pltpu.VMEM((24 * rows, columns), jnp.bfloat16)],
        flops=flops,
    )
    far = [(kz, kx, ky) for kx, ky in (*SIDES, (0, 0)) for kz in (2, 3)]
    near = [(kz, kx, ky) for kz in (1, 0) for kx, ky in (*SIDES, (0, 0))]
    sent, left, right = kernel_call(
        functools.partial(attend_kernel, [place for _, place in late], far[:2], rows, head, grad_scale),
        [bfloat((2 * rows, columns))] + [bfloat((tokens, columns))] * 2,
        "attend",
        (*[piece for piece, _ in late], acts, cots, documents, acts_t, cots_t, front, back),
        scratch=[pltpu.VMEM((24 * rows, columns), jnp.bfloat16)],
        flops=flops,
    )

    def terms(blocks, kc, dtype):
        return kernel_call(
            functools.partial(terms_kernel, blocks, kc, rows, grad_scale),
            [dtype((len(blocks) * rows, columns))],
            "terms",
            (acts_t, cots_t, left, right),
            flops=flops * len(blocks) // 32,
        )[0]

    def other_core(value):
        return hop(value, 0, 0, 0, 1)

    sent = other_core(sent)
    rest = other_core(terms(far[2:], 1, bfloat))
    near_other = other_core(terms(near, 1, bfloat))
    mine = terms(far, 0, float32)
    diagonal = add(mine[: 2 * rows], sent)
    along_x, along_y, total = cut(add(mine[2 * rows :], rest), 3)
    total = add(total, *[hop(low(part), 0, *side, 0) for part, side in zip((diagonal, along_x, along_y), SIDES)])
    total_2, total_3 = cut(total, 2)
    one, zero = cut(add(terms(near, 0, float32), near_other), 2)
    *parts, gradient = cut(add(zero, hop(low(one), 1, 0, 0, 0)), 4)
    arrived = [hop(low(part), 0, *side, 0) for part, side in zip(parts, SIDES)]
    arrived += [hop(low(total_2), 2, 0, 0, 0), hop(low(total_3), 3, 0, 0, 0)]
    gradient = add(gradient, *arrived)
    primary_new, first_new, second_new = adam(gradient, primary, first_moment, second_moment)
    copy_new = lax.all_gather(primary_new.astype(jnp.bfloat16), "rep", axis=0, tiled=True)
    return primary_new, first_new, second_new, copy_new


def chosen_body(activations, cotangent, documents, weight_copy, primary, first_moment, second_moment):
    blocks = lax.axis_size("grp") == 8 and lax.axis_size("rep") == 4
    tiled = primary.shape[0] % 16 == 0 and activations.shape[1] % 16 == 0
    args = (activations, cotangent, documents, weight_copy, primary, first_moment, second_moment)
    return block_body(*args) if blocks and tiled else plain_body(*args)


def solution(mesh):
    in_specs = (
        P(("grp", "rep"), None, None),
        P(("grp", "rep"), None, None),
        P(("grp", "rep"), None),
        P("grp", None),
        P(("grp", "rep"), None),
        P(("grp", "rep"), None),
        P(("grp", "rep"), None),
    )
    out_specs = (
        P(("grp", "rep"), None),
        P(("grp", "rep"), None),
        P(("grp", "rep"), None),
        P("grp", None),
    )
    return jax.shard_map(chosen_body, mesh=mesh, in_specs=in_specs, out_specs=out_specs, check_vma=False)
```
